32 devices in a mesh: groups: 2 (over x), fsdp: 16 (over z, y, core).
Axes of the slice: x: 2, y: 2, z: 4, core: 2. Of those that a mesh axis runs over, the one named last changes fastest.
Arguments:
- acts: bfloat16 [8192, 8192], P(('groups', 'fsdp')), parts along dimension 0, may hold values from -6 to 6
- cotangent: bfloat16 [4096, 1024], P(('groups', 'fsdp')), parts along dimension 0, may hold values from -6 to 6
- plan: int32 [64], P('groups'), parts along dimension 0, may hold values from -1 to 15, as said below
- source_block_length: int32 [64], P('groups'), parts along dimension 0, may hold values from 0 to 128, as said below
- source_block_job: int32 [64], P('groups'), parts along dimension 0, may hold values from 0 to 7
- frozen_value_weight: bfloat16 [8192, 1024], P('fsdp'), may hold values from -0.0625 to 0.0625
- adapter_down_weight: bfloat16 [16384, 128], P(('groups', 'fsdp')), parts along dimension 0, may hold values from -0.0625 to 0.0625
- adapter_up_weight: bfloat16 [256, 1024], P('groups'), parts along dimension 0, may hold values from -0.1875 to 0.1875
Outputs:
- values: bfloat16 [4096, 1024], P(('groups', 'fsdp')), parts along dimension 0
- layer_input_gradient: bfloat16 [8192, 8192], P(('groups', 'fsdp')), parts along dimension 0
- down_grad: float32 [16384, 128], P(('groups', 'fsdp')), parts along dimension 0
- up_weight_gradient: float32 [256, 1024], P('groups'), parts along dimension 0
The draws below stay inside these ranges and needn't reach their ends.
There are 2 independent parts, one for each index of `groups`. The reference program is written for one: setup_inputs(seed, part) draws one part's arguments, and reference() takes and returns one part's arrays. A program takes and returns all parts, laid end to end along the dimension named above; an argument that names none is the same for every part. Nothing has to cross between parts.
Inputs may be any that keep to these rules, and one draw needn't show every extreme that they name: Device i holds source slots i * 2 to i * 2 + 1. plan is -1 exactly where source_block_length is 0; otherwise it is i or i + 1, and no two slots share a value, so each balanced block receives at most one slot. Which slot of a device holds which block varies. `source_block_length`: live tokens are the first ones of a block; some block is full in every draw.
All inputs are finite; a program needn't handle non-finite values.
Results may differ from the reference program's by a relative error of at most 0.0031.
Values may be sent and summed in bfloat16 or wider, within the bound.
A program may use at most 128 MiB of HBM per device.

```python
import jax
import jax.numpy as jnp
from jax import lax

MODEL_WIDTH = 8192
ADAPTER_RANK = 16
ADJUST_JOBS = 8
BLK = 128
SLOTS = 2
VALUE_PROJ_WIDTH = 1024
N_FSDP = 16


def block_layout(key):
    devices = N_FSDP
    key_kind, key_force, key_order = jax.random.split(key, 3)
    kinds = jax.random.randint(key_kind, (devices,), 0, 8)
    forced = jax.random.randint(key_force, (), 0, devices - 1)
    indices = jnp.arange(devices, dtype=jnp.int32)
    kinds = jnp.where(indices == forced, 0, kinds)
    kinds = jnp.where(indices == forced + 1, 5, kinds)
    kinds = jnp.where(indices == devices - 1, 5, kinds)
    keeps = kinds < 5
    takes_left = (kinds >= 5) & (kinds < 7) & (indices > 0)
    sends_right = jnp.concatenate([takes_left[1:], jnp.zeros((1,), dtype=bool)])
    order_bit = jax.random.randint(key_order, (devices,), 0, 2)
    own_place = order_bit
    right_place = jnp.where(keeps, 1 - order_bit, order_bit)
    entries = []
    for place in range(SLOTS):
        entry = jnp.where(keeps & (own_place == place), indices, jnp.where(sends_right & (right_place == place), indices + 1, -1))
        entries.append(entry)
    plan = jnp.stack(entries, 1).reshape(-1).astype(jnp.int32)
    forced_slot = forced * SLOTS + own_place[forced]
    return (plan, forced_slot)


def draw_plan(key, part):
    plan, forced_slot = block_layout(key)
    return plan


def draw_source_block_length(key, part):
    plan, forced_slot = block_layout(key)
    key = jax.random.fold_in(key, 13)
    lengths = jax.random.randint(key, plan.shape, 1, BLK + 1)
    slot_ids = jnp.arange(plan.shape[0], dtype=jnp.int32)
    lengths = jnp.where(slot_ids == forced_slot, BLK, lengths)
    return jnp.where(plan >= 0, lengths, 0).astype(jnp.int32)


def place_ends(values, key, least, top_value):
    spot = [jax.random.randint(jax.random.fold_in(key, axis), (), 0, length) for axis, length in enumerate(values.shape)]
    main_axis = values.shape.index(max(values.shape))
    neighbour = spot[:main_axis] + [(spot[main_axis] + 1) % values.shape[main_axis]] + spot[main_axis + 1:]
    return values.at[tuple(spot)].set(least).at[tuple(neighbour)].set(top_value)


def steps_of(stream_key, extent, cuts, smallest, top_value):
    level, own = 1.0, jax.random.fold_in(stream_key, 6)
    for position, parts in cuts:
        heights = jnp.exp(jax.random.uniform(jax.random.fold_in(own, position), (parts,), jnp.float32, smallest / len(cuts), top_value / len(cuts)))
        level = level * jnp.repeat(heights, extent[position] // parts).reshape([-1 if axis == position else 1 for axis in range(len(extent))])
    return level


def bell_draw(key, shape, deviation, limit, cuts=(), held_as=jnp.bfloat16):
    values = jax.random.normal(key, shape, jnp.float32) * deviation
    if len(cuts) > 0:
        values = steps_of(key, shape, cuts, -0.22, 0.18) * values
    return jnp.clip(values, min=-limit, max=limit).astype(held_as)


def setup_inputs(seed: int = 0, part: int = 0) -> dict:
    arg_keys = jax.random.split(jax.random.key(seed), 9)
    part_splits = jax.random.split(jax.random.fold_in(arg_keys[8], part), 9)
    return {
        "acts": bell_draw(part_splits[0], (N_FSDP * SLOTS * BLK, MODEL_WIDTH), 1.0, 6.0, ((0, 16),)),
        "cotangent": bell_draw(part_splits[1], (N_FSDP * BLK, VALUE_PROJ_WIDTH), 1.0, 6.0, ((0, 16),)),
        "plan": draw_plan(jax.random.fold_in(jax.random.fold_in(arg_keys[8], part), 71), part),
        "source_block_length": draw_source_block_length(jax.random.fold_in(jax.random.fold_in(arg_keys[8], part), 71), part),
        "source_block_job": place_ends(jax.random.randint(part_splits[4], (N_FSDP * SLOTS,), 0, ADJUST_JOBS), jax.random.fold_in(part_splits[4], 1), 0, ADJUST_JOBS - 1).astype(jnp.int32),
        "frozen_value_weight": bell_draw(arg_keys[5], (MODEL_WIDTH, VALUE_PROJ_WIDTH), MODEL_WIDTH ** -0.5, 0.0625, ((0, 16),)),
        "adapter_down_weight": bell_draw(part_splits[6], (MODEL_WIDTH, ADJUST_JOBS * ADAPTER_RANK), MODEL_WIDTH ** -0.5, 0.0625, ((0, 16),)),
        "adapter_up_weight": bell_draw(part_splits[7], (ADJUST_JOBS * ADAPTER_RANK, VALUE_PROJ_WIDTH), VALUE_PROJ_WIDTH ** -0.5, 0.1875),
    }


ADAPTER_SCALE = 2.0


def contract_trailing(left, right):
    return lax.dot_general(left, right, (((1,), (1,)), ((), ())), preferred_element_type=jnp.float32)


def contract_leading(left, right):
    return lax.dot_general(left, right, (((0,), (0,)), ((), ())), preferred_element_type=jnp.float32)


def reference(acts, cotangent, plan, source_block_length, source_block_job, frozen_value_weight, adapter_down_weight, adapter_up_weight):
    slot_total = plan.shape[0]
    live_slots = plan >= 0
    target = jnp.where(live_slots, plan, 0).astype(jnp.int32)
    positions = jnp.arange(BLK, dtype=jnp.int32)
    live_token_mask = (positions[None, :] < source_block_length[:, None]).astype(jnp.float32).reshape(-1)
    dy_blocks = cotangent.reshape(N_FSDP, BLK, VALUE_PROJ_WIDTH)[target].reshape(slot_total * BLK, VALUE_PROJ_WIDTH)
    source_output_gradient = (dy_blocks.astype(jnp.float32) * live_token_mask[:, None]).astype(jnp.bfloat16)
    column_span = jnp.arange(ADJUST_JOBS * ADAPTER_RANK, dtype=jnp.int32) // ADAPTER_RANK
    job_rows = jnp.repeat(source_block_job, BLK)
    job_column_span = (column_span[None, :] == job_rows[:, None]).astype(jnp.float32)
    reduced_rank_state = (jnp.dot(acts, adapter_down_weight, preferred_element_type=jnp.float32) * job_column_span).astype(jnp.bfloat16)
    output_rows = jnp.dot(acts, frozen_value_weight, preferred_element_type=jnp.float32)
    output_rows = output_rows + ADAPTER_SCALE * jnp.dot(reduced_rank_state, adapter_up_weight, preferred_element_type=jnp.float32)
    output_rows = (output_rows * live_token_mask[:, None]).astype(jnp.bfloat16).reshape(slot_total, BLK, VALUE_PROJ_WIDTH)
    values = jnp.zeros((N_FSDP, BLK, VALUE_PROJ_WIDTH), jnp.bfloat16).at[target].add(output_rows)
    hidden_state = (ADAPTER_SCALE * contract_trailing(source_output_gradient, adapter_up_weight) * job_column_span).astype(jnp.bfloat16)
    layer_input_gradient = (contract_trailing(source_output_gradient, frozen_value_weight) + contract_trailing(hidden_state, adapter_down_weight)).astype(jnp.bfloat16)
    down_grad = contract_leading(acts, hidden_state)
    up_weight_gradient = ADAPTER_SCALE * contract_leading(reduced_rank_state, source_output_gradient)
    return values.reshape(N_FSDP * BLK, VALUE_PROJ_WIDTH), layer_input_gradient, down_grad, up_weight_gradient
```

```python
import functools

import jax
import jax.numpy as jnp
from jax import lax
from jax.experimental import pallas as pl
from jax.experimental.pallas import tpu as pltpu
from jax.sharding import PartitionSpec as P

ADAPTER_RANK = 16
BLK = 128
ADAPTER_SCALE = 2.0
REDUCERS = 8
MESH = pl.DeviceIdType.MESH
F32 = jnp.float32
BF16 = jnp.bfloat16


def dot(left, right, left_dim, right_dim):
    return lax.dot_general(
        left, right, (((left_dim,), (right_dim,)), ((), ())), preferred_element_type=F32
    )


def kernel(
    n,
    plan,
    length,
    job,
    codes,
    acts_in,
    cot,
    w_in,
    d_in,
    up,
    values_out,
    grads_out,
    down_out,
    up_out,
    acts,
    wbuf,
    dbuf,
    cot_right,
    dy,
    hidden,
    acc,
    gbuf,
    pbuf,
    pgot,
    ubuf,
    ugot,
    utotal,
    vsend,
    vgot,
    local_sem,
    out_sem,
    cot_sem,
    val_sem,
    w_recv,
    w_send,
    wz_send,
    d_recv,
    d_send,
    dz_send,
    p_send,
    p_recv,
    u_send,
    u_recv,
    t_send,
    t_recv,
):
    nz = n // 4
    rows = w_in.shape[0]
    piece = rows // 4
    tokens = acts.shape[0]
    rank2 = 2 * ADAPTER_RANK
    g = lax.axis_index("groups")
    me = lax.axis_index("fsdp")
    z, y, c = me // 4, (me // 2) % 2, me % 2
    x = g % 2
    to_x = (g + 1 - 2 * x, me)
    to_y = (g, me + 2 - 4 * y)
    to_s = (g, me + 1 - 2 * c)
    to_up = (g, me + 4)
    to_dn = (g, me - 4)

    local = [
        pltpu.make_async_copy(
            w_in, wbuf.at[pl.ds(pl.multiple_of(me * rows, rows), rows)], local_sem.at[0]
        ),
        pltpu.make_async_copy(
            d_in, dbuf.at[pl.ds(pl.multiple_of(me * rows, rows), rows)], local_sem.at[1]
        ),
        pltpu.make_async_copy(acts_in, acts, local_sem.at[2]),
    ]
    for copy in local:
        copy.start()

    barrier = pltpu.get_barrier_semaphore()

    def greet(t, carry):
        pl.semaphore_signal(
            barrier, inc=1, device_id=(g, lax.rem(me + t, n)), device_id_type=MESH
        )
        return carry

    lax.fori_loop(1, n, greet, 0)
    pl.semaphore_signal(barrier, inc=1, device_id=to_x, device_id_type=MESH)
    pl.semaphore_wait(barrier, n)

    def shard_id(z_, y_, c_):
        return z_ * 4 + y_ * 2 + c_

    def w_copy(s, h, q, send, device):
        part = wbuf.at[pl.ds(pl.multiple_of(s * rows + h * 2 * piece + q * piece, piece), piece)]
        return pltpu.make_async_remote_copy(
            src_ref=part,
            dst_ref=part,
            send_sem=send,
            recv_sem=w_recv.at[s * 4 + h * 2 + q],
            device_id=device,
            device_id_type=MESH,
        )

    def d_copy(s, send, device):
        part = dbuf.at[pl.ds(pl.multiple_of(s * rows, rows), rows)]
        return pltpu.make_async_remote_copy(
            src_ref=part,
            dst_ref=part,
            send_sem=send,
            recv_sem=d_recv.at[s],
            device_id=device,
            device_id_type=MESH,
        )

    def w_wait(s, h, q):
        w_copy(s, h, q, w_send.at[0], to_x).wait_recv()

    def d_wait(s):
        d_copy(s, d_send.at[0], to_y).wait_recv()

    cot_copy = pltpu.make_async_remote_copy(
        src_ref=cot,
        dst_ref=cot_right,
        send_sem=cot_sem.at[0],
        recv_sem=cot_sem.at[1],
        device_id=(g, jnp.maximum(me - 1, 0)),
        device_id_type=MESH,
    )

    @pl.when(me > 0)
    def _():
        cot_copy.start()

    local[1].wait()

    @pl.when(z < nz - 1)
    def _():
        d_copy(me, dz_send.at[0], to_up).start()

    @pl.when(z > 0)
    def _():
        d_copy(me, dz_send.at[nz], to_dn).start()

    d_copy(me, d_send.at[0], to_y).start()
    d_copy(me, d_send.at[1], to_s).start()
    local[0].wait()
    for q in range(2):

        @pl.when(z < nz - 1)
        def _():
            w_copy(me, x, q, wz_send.at[q], to_up).start()

        @pl.when(z > 0)
        def _():
            w_copy(me, x, q, wz_send.at[2 * nz + q], to_dn).start()

        w_copy(me, x, q, w_send.at[1], to_y).start()
    for h in range(2):
        for q in range(2):
            w_copy(me, h, q, w_send.at[2], to_s).start()

    @pl.when(me == n - 1)
    def _():
        cot_right[...] = jnp.zeros_like(cot_right)

    @pl.when(me < n - 1)
    def _():
        cot_copy.wait_recv()

    token = lax.broadcasted_iota(jnp.int32, (BLK, 1), 0)
    column = lax.broadcasted_iota(jnp.int32, (BLK, up.shape[0]), 1)
    jobmask = []
    live = []
    for b in range(2):
        p = plan[2 * me + b]
        jobs = job[2 * me + b]
        live.append(token < length[2 * me + b])
        own = live[b] & (p == me)
        right = live[b] & (p == me + 1)
        zero = jnp.zeros((BLK, cot.shape[1]), F32)
        block = jnp.where(
            own,
            cot[...].astype(F32),
            jnp.where(right, cot_right[...].astype(F32), zero),
        ).astype(BF16)
        dy[pl.ds(b * BLK, BLK), :] = block
        jobmask.append((column // ADAPTER_RANK == jobs).astype(F32))
        hidden[pl.ds(b * BLK, BLK), :] = (
            ADAPTER_SCALE * dot(block, up[...], 1, 1) * jobmask[b]
        ).astype(BF16)

    line = lax.broadcasted_iota(jnp.int32, (rank2, up.shape[0]), 0)
    where_col = lax.broadcasted_iota(jnp.int32, (rank2, up.shape[0]), 1)
    line_job = jnp.where(line < ADAPTER_RANK, job[2 * me], job[2 * me + 1])
    pick = (where_col == line_job * ADAPTER_RANK + line % ADAPTER_RANK).astype(F32).astype(BF16)
    same_slot = (
        lax.broadcasted_iota(jnp.int32, (rank2, tokens), 0) // ADAPTER_RANK
        == lax.broadcasted_iota(jnp.int32, (rank2, tokens), 1) // BLK
    )
    hidden_rows = jnp.where(same_slot, dot(pick, hidden[...], 1, 1), 0.0).astype(BF16)
    local[2].wait()

    def cols(s):
        return pl.ds(pl.multiple_of(s * rows, rows), rows)

    def p_part(s, carry):
        pbuf[s] = dot(hidden_rows, acts[:, cols(s)], 1, 0).astype(BF16)
        return carry

    lax.fori_loop(0, n, p_part, 0)

    def p_copy(t):
        other = lax.rem(me + t, n)
        return pltpu.make_async_remote_copy(
            src_ref=pbuf.at[other],
            dst_ref=pgot.at[me],
            send_sem=p_send.at[0],
            recv_sem=p_recv.at[me],
            device_id=(g, other),
            device_id_type=MESH,
        )

    def p_start(t, carry):
        p_copy(t).start()
        return carry

    for d in range(1, nz):

        @pl.when(z >= d)
        def _():
            s = shard_id(z - d, y, c)
            d_wait(s)

            @pl.when(z < nz - 1)
            def _():
                d_copy(s, dz_send.at[d], to_up).start()

            d_copy(s, d_send.at[0], to_y).start()
            d_copy(s, d_send.at[1], to_s).start()

        @pl.when(z + d < nz)
        def _():
            s = shard_id(z + d, y, c)
            d_wait(s)

            @pl.when(z > 0)
            def _():
                d_copy(s, dz_send.at[nz + d], to_dn).start()

            d_copy(s, d_send.at[0], to_y).start()
            d_copy(s, d_send.at[1], to_s).start()

    lax.fori_loop(1, n, p_start, 0)
    pgot[me] = pbuf[me]

    def z_part(d):
        for up_way in (True, False):

            @pl.when(z >= d if up_way else z + d < nz)
            def _():
                s = shard_id(z - d if up_way else z + d, y, c)
                for q in range(2):
                    w_wait(s, x, q)

                    @pl.when(z < nz - 1 if up_way else z > 0)
                    def _():
                        w_copy(
                            s,
                            x,
                            q,
                            wz_send.at[(0 if up_way else 2 * nz) + 2 * d + q],
                            to_up if up_way else to_dn,
                        ).start()

                    w_copy(s, x, q, w_send.at[0], to_x).start()
                    w_copy(s, x, q, w_send.at[1], to_y).start()
                    w_copy(s, x, q, w_send.at[2], to_s).start()

    def xy_part(d):
        for up_way in (True, False):

            @pl.when(z >= d if up_way else z + d < nz)
            def _():
                z_ = z - d if up_way else z + d
                a = shard_id(z_, y, c)
                b = shard_id(z_, 1 - y, c)
                for q in range(2):
                    w_wait(a, 1 - x, q)
                    if q == 0:
                        w_copy(a, 1 - x, q, w_send.at[1], to_y).start()
                    w_copy(a, 1 - x, q, w_send.at[2], to_s).start()
                    w_wait(b, x, q)
                    if q == 1:
                        w_copy(b, x, q, w_send.at[0], to_x).start()
                    w_copy(b, x, q, w_send.at[2], to_s).start()
                for q in range(2):
                    w_wait(b, 1 - x, q)
                    w_copy(b, 1 - x, q, w_send.at[2], to_s).start()

    first = shard_id(z, 1 - y, c)
    for q in range(2):
        w_wait(first, x, q)
        w_copy(first, x, q, w_send.at[0], to_x).start()
        w_copy(first, x, q, w_send.at[2], to_s).start()

    for z_ in range(nz):
        s = shard_id(z_, 1 - y, c)
        d_wait(s)
        d_copy(s, d_send.at[1], to_s).start()

    def d_sib(i, carry):
        d_wait(2 * i + 1 - c)
        return carry

    lax.fori_loop(0, n // 2, d_sib, 0)

    acc[...] = jnp.zeros_like(acc)

    def low_part(s, total):
        return total + dot(acts[:, cols(s)], dbuf[cols(s), :], 1, 0)

    low = lax.fori_loop(0, n, low_part, jnp.zeros((tokens, up.shape[0]), F32))
    low = (low * jnp.concatenate(jobmask, 0)).astype(BF16)
    low_rows = jnp.where(same_slot, dot(pick, low, 1, 1), 0.0).astype(BF16)
    up_part = (ADAPTER_SCALE * dot(low_rows, dy[...], 1, 0)).astype(BF16)
    width = up_part.shape[1] // REDUCERS
    every = n // REDUCERS
    for k in range(REDUCERS):
        ubuf[k] = up_part[:, k * width : (k + 1) * width]
    for k in range(REDUCERS):

        @pl.when(me == k * every)
        def _():
            ugot[me] = ubuf[k]

        @pl.when(me != k * every)
        def _():
            pltpu.make_async_remote_copy(
                src_ref=ubuf.at[k],
                dst_ref=ugot.at[me],
                send_sem=u_send.at[k],
                recv_sem=u_recv.at[me],
                device_id=(g, k * every),
                device_id_type=MESH,
            ).start()

    def compute(s):
        a = acts[:, cols(s)]
        w = wbuf[cols(s), :]
        acc[...] += dot(a, w, 1, 0)
        gbuf[:, cols(s)] = (dot(dy[...], w, 1, 1) + dot(hidden[...], dbuf[cols(s), :], 1, 1)).astype(BF16)
        pltpu.make_async_copy(gbuf.at[:, cols(s)], grads_out.at[:, cols(s)], out_sem.at[0]).start()

    def slab(d, ways):
        def one(i, carry):
            down_way, j = i // 4, i % 4
            z_ = jnp.where(down_way == 1, z + d, z - d)
            y_ = lax.rem(y + j, 2)
            c_ = lax.rem(c + j // 2, 2)

            @pl.when((z_ >= 0) & (z_ < nz))
            def _():
                s = shard_id(z_, y_, c_)

                @pl.when(c_ != c)
                def _():
                    for h in range(2):
                        for q in range(2):
                            w_wait(s, h, q)

                compute(s)

            return carry

        lax.fori_loop(0, 4 * ways, one, 0)

    if nz > 1:
        z_part(1)
    for q in range(2):
        w_wait(first, 1 - x, q)
        w_copy(first, 1 - x, q, w_send.at[2], to_s).start()
    slab(0, 1)

    def t_copy(k, other):
        return pltpu.make_async_remote_copy(
            src_ref=utotal.at[k],
            dst_ref=utotal.at[k],
            send_sem=t_send.at[0],
            recv_sem=t_recv.at[k],
            device_id=(g, other),
            device_id_type=MESH,
        )

    hot = (
        lax.broadcasted_iota(jnp.int32, (up.shape[0], codes.shape[1]), 0) == codes[...]
    ).astype(F32).astype(BF16)

    @pl.when(me % every == 0)
    def _():
        def u_wait(t, carry):
            other = lax.rem(me + t, n)
            pltpu.make_async_remote_copy(
                src_ref=ubuf.at[0],
                dst_ref=ugot.at[other],
                send_sem=u_send.at[0],
                recv_sem=u_recv.at[other],
                device_id=(g, other),
                device_id_type=MESH,
            ).wait_recv()
            return carry

        lax.fori_loop(1, n, u_wait, 0)
        k = me // every
        utotal[k] = dot(hot, ugot[...].reshape(n * rank2, width), 1, 0).astype(BF16)

        def t_start(t, carry):
            t_copy(k, lax.rem(me + t, n)).start()
            return carry

        lax.fori_loop(1, n, t_start, 0)

    def p_wait(t, carry):
        other = lax.rem(me + t, n)
        pltpu.make_async_remote_copy(
            src_ref=pbuf.at[0],
            dst_ref=pgot.at[other],
            send_sem=p_send.at[0],
            recv_sem=p_recv.at[other],
            device_id=(g, other),
            device_id_type=MESH,
        ).wait_recv()
        return carry

    lax.fori_loop(1, n, p_wait, 0)
    down_out[...] = dot(pgot[...].reshape(n * rank2, rows), hot, 0, 1)

    def step(d, carry):
        @pl.when(d + 1 < nz)
        def _():
            z_part(d + 1)

        xy_part(d)
        slab(d, 2)
        return carry

    lax.fori_loop(1, nz, step, 0)

    whole = acc[...] + ADAPTER_SCALE * dot(low, up[...], 1, 0)
    keep = jnp.zeros((BLK, up.shape[1]), F32)
    give = keep
    for b in range(2):
        p = plan[2 * me + b]
        block = whole[b * BLK : (b + 1) * BLK]
        keep = jnp.where(live[b] & (p == me), block, keep)
        give = jnp.where(live[b] & (p == me + 1), block, give)
    vsend[...] = give.astype(BF16)
    val_copy = pltpu.make_async_remote_copy(
        src_ref=vsend,
        dst_ref=vgot,
        send_sem=val_sem.at[0],
        recv_sem=val_sem.at[1],
        device_id=(g, jnp.minimum(me + 1, n - 1)),
        device_id_type=MESH,
    )

    @pl.when(me < n - 1)
    def _():
        val_copy.start()

    for k in range(REDUCERS):

        @pl.when(me != k * every)
        def _():
            t_copy(k, k * every).wait_recv()

        up_out[:, k * width : (k + 1) * width] = utotal[k].astype(F32)

    def drain(ref, sem):
        pltpu.make_async_copy(ref, ref, sem).wait()

    drain(wbuf.at[pl.ds(0, (3 * nz - 1) * piece)], w_send.at[0])
    drain(wbuf.at[pl.ds(0, (3 * nz - 1) * piece)], w_send.at[1])
    drain(wbuf.at[pl.ds(0, n // 2 * rows)], w_send.at[2])
    drain(dbuf.at[pl.ds(0, nz * rows)], d_send.at[0])
    drain(dbuf.at[pl.ds(0, n // 2 * rows)], d_send.at[1])
    drain(pbuf.at[pl.ds(0, n - 1)], p_send.at[0])

    for d in range(nz):
        for up_way in (True, False):

            @pl.when((z >= d) & (z < nz - 1) if up_way else (z + d < nz) & (z > 0))
            def _():
                s = shard_id(z - d if up_way else z + d, y, c)
                base = 0 if up_way else nz
                d_copy(s, dz_send.at[base + d], to_y).wait_send()
                for q in range(2):
                    w_copy(s, x, q, wz_send.at[2 * base + 2 * d + q], to_y).wait_send()

    for k in range(REDUCERS):

        @pl.when(me != k * every)
        def _():
            drain(ubuf.at[k], u_send.at[k])

    @pl.when(me % every == 0)
    def _():
        drain(dbuf.at[pl.ds(0, (n - 1) * width)], t_send.at[0])

    @pl.when(me > 0)
    def _():
        cot_copy.wait_send()

    pltpu.make_async_copy(gbuf, grads_out, out_sem.at[0]).wait()

    @pl.when(me < n - 1)
    def _():
        val_copy.wait_send()

    @pl.when(me == 0)
    def _():
        values_out[...] = keep.astype(BF16)

    @pl.when(me > 0)
    def _():
        val_copy.wait_recv()
        values_out[...] = (keep + vgot[...].astype(F32)).astype(BF16)


def body(
    n,
    acts,
    cotangent,
    plan,
    source_block_length,
    source_block_job,
    frozen_value_weight,
    adapter_down_weight,
    adapter_up_weight,
):
    tokens, features = acts.shape
    rows, out_width = frozen_value_weight.shape
    job_columns = adapter_down_weight.shape[1]
    rank2 = 2 * ADAPTER_RANK
    width = out_width // REDUCERS
    codes = (
        source_block_job[:, None] * ADAPTER_RANK + jnp.arange(ADAPTER_RANK, dtype=jnp.int32)[None]
    ).reshape(1, -1)
    smem = pl.BlockSpec(memory_space=pltpu.SMEM)
    vmem = pl.BlockSpec(memory_space=pltpu.VMEM)
    anywhere = pl.BlockSpec(memory_space=pl.ANY)
    dma = pltpu.SemaphoreType.DMA
    nz = n // 4
    return pl.pallas_call(
        functools.partial(kernel, n),
        out_shape=(
            jax.ShapeDtypeStruct((BLK, out_width), BF16),
            jax.ShapeDtypeStruct((tokens, features), BF16),
            jax.ShapeDtypeStruct((rows, job_columns), F32),
            jax.ShapeDtypeStruct((job_columns, out_width), F32),
        ),
        in_specs=[smem, smem, smem, vmem, anywhere, vmem, anywhere, anywhere, vmem],
        out_specs=(vmem, anywhere, vmem, vmem),
        scratch_shapes=[
            pltpu.VMEM((tokens, features), BF16),
            pltpu.VMEM((n * rows, out_width), BF16),
            pltpu.VMEM((n * rows, job_columns), BF16),
            pltpu.VMEM((BLK, out_width), BF16),
            pltpu.VMEM((tokens, out_width), BF16),
            pltpu.VMEM((tokens, job_columns), BF16),
            pltpu.VMEM((tokens, out_width), F32),
            pltpu.VMEM((tokens, features), BF16),
            pltpu.VMEM((n, rank2, rows), BF16),
            pltpu.VMEM((n, rank2, rows), BF16),
            pltpu.VMEM((REDUCERS, rank2, width), BF16),
            pltpu.VMEM((n, rank2, width), BF16),
            pltpu.VMEM((REDUCERS, job_columns, width), BF16),
            pltpu.VMEM((BLK, out_width), BF16),
            pltpu.VMEM((BLK, out_width), BF16),
            dma((3,)),
            dma((1,)),
            dma((2,)),
            dma((2,)),
            dma((n * 4,)),
            dma((3,)),
            dma((4 * nz,)),
            dma((n,)),
            dma((2,)),
            dma((2 * nz,)),
            dma((1,)),
            dma((n,)),
            dma((REDUCERS,)),
            dma((n,)),
            dma((1,)),
            dma((REDUCERS,)),
        ],
        compiler_params=pltpu.CompilerParams(
            collective_id=0, has_side_effects=True, vmem_limit_bytes=56 * 1024 * 1024
        ),
        cost_estimate=pl.CostEstimate(
            flops=4 * tokens * features * out_width,
            bytes_accessed=4 * tokens * features,
            transcendentals=0,
        ),
    )(
        plan,
        source_block_length,
        source_block_job,
        codes,
        acts,
        cotangent,
        frozen_value_weight,
        adapter_down_weight,
        adapter_up_weight,
    )


def solution(mesh):
    placed = (
        P(("groups", "fsdp"), None),
        P(("groups", "fsdp"), None),
        P("groups"),
        P("groups"),
        P("groups"),
        P("fsdp", None),
        P(("groups", "fsdp"), None),
        P("groups", None),
    )
    return jax.shard_map(
        functools.partial(body, mesh.shape["fsdp"]),
        mesh=mesh,
        in_specs=placed,
        out_specs=(
            P(("groups", "fsdp"), None),
            P(("groups", "fsdp"), None),
            P(("groups", "fsdp"), None),
            P("groups", None),
        ),
        check_vma=False,
    )
```

```python
import functools

import jax
import jax.numpy as jnp
from jax import lax
from jax.experimental import pallas as pl
from jax.experimental.pallas import tpu as pltpu
from jax.sharding import PartitionSpec as P

ADAPTER_RANK = 16
BLK = 128
ADAPTER_SCALE = 2.0
REDUCERS = 8
MESH = pl.DeviceIdType.MESH
F32 = jnp.float32
BF16 = jnp.bfloat16


def dot(left, right, left_dim, right_dim):
    return lax.dot_general(
        left, right, (((left_dim,), (right_dim,)), ((), ())), preferred_element_type=F32
    )


def kernel(
    n,
    plan,
    length,
    job,
    codes,
    acts_in,
    cot,
    w_in,
    d_in,
    up,
    values_out,
    gbuf,
    down_out,
    up_out,
    acts,
    wbuf,
    dsend,
    dgot,
    cot_right,
    dy,
    hidden,
    acc,
    pbuf,
    pgot,
    ubuf,
    ugot,
    utotal,
    vsend,
    vgot,
    local_sem,
    cot_sem,
    val_sem,
    w_recv,
    w_send,
    wz_send,
    d_recv,
    d_send,
    p_send,
    p_recv,
    u_send,
    u_recv,
    t_send,
    t_recv,
):
    nz = n // 4
    rows = w_in.shape[0]
    piece = rows // 4
    tokens = acts.shape[0]
    rank2 = 2 * ADAPTER_RANK
    g = lax.axis_index("groups")
    me = lax.axis_index("fsdp")
    z, y, c = me // 4, (me // 2) % 2, me % 2
    x = g % 2
    to_x = (g + 1 - 2 * x, me)
    to_y = (g, me + 2 - 4 * y)
    to_s = (g, me + 1 - 2 * c)
    to_up = (g, me + 4)
    to_dn = (g, me - 4)

    local = [
        pltpu.make_async_copy(
            w_in, wbuf.at[pl.ds(pl.multiple_of(me * rows, rows), rows)], local_sem.at[0]
        ),
        pltpu.make_async_copy(acts_in, acts, local_sem.at[1]),
    ]
    for copy in local:
        copy.start()

    barrier = pltpu.get_barrier_semaphore()

    def greet(t, carry):
        pl.semaphore_signal(
            barrier, inc=1, device_id=(g, lax.rem(me + t, n)), device_id_type=MESH
        )
        return carry

    lax.fori_loop(1, n, greet, 0)
    pl.semaphore_signal(barrier, inc=1, device_id=to_x, device_id_type=MESH)
    pl.semaphore_wait(barrier, n)

    def shard_id(z_, y_, c_):
        return z_ * 4 + y_ * 2 + c_

    def w_copy(s, h, q, send, device):
        part = wbuf.at[pl.ds(pl.multiple_of(s * rows + h * 2 * piece + q * piece, piece), piece)]
        return pltpu.make_async_remote_copy(
            src_ref=part,
            dst_ref=part,
            send_sem=send,
            recv_sem=w_recv.at[s * 4 + h * 2 + q],
            device_id=device,
            device_id_type=MESH,
        )

    def w_wait(s, h, q):
        w_copy(s, h, q, w_send.at[0], to_x).wait_recv()

    cot_copy = pltpu.make_async_remote_copy(
        src_ref=cot,
        dst_ref=cot_right,
        send_sem=cot_sem.at[0],
        recv_sem=cot_sem.at[1],
        device_id=(g, jnp.maximum(me - 1, 0)),
        device_id_type=MESH,
    )

    @pl.when(me > 0)
    def _():
        cot_copy.start()

    local[0].wait()
    for q in range(2):

        @pl.when(z < nz - 1)
        def _():
            w_copy(me, x, q, wz_send.at[q], to_up).start()

        @pl.when(z > 0)
        def _():
            w_copy(me, x, q, wz_send.at[2 * nz + q], to_dn).start()

        w_copy(me, x, q, w_send.at[1], to_y).start()
    for h in range(2):
        for q in range(2):
            w_copy(me, h, q, w_send.at[2], to_s).start()

    hot = (
        lax.broadcasted_iota(jnp.int32, (up.shape[0], codes.shape[1]), 0) == codes[...]
    ).astype(F32).astype(BF16)

    def cols(s):
        return pl.ds(pl.multiple_of(s * rows, rows), rows)

    dsend[...] = dot(hot, d_in[...], 0, 1).astype(BF16).reshape(n, rank2, rows)
    dgot[me] = dsend[me]

    def exchange(src, dst, send, recv, t):
        other = lax.rem(me + t, n)
        return pltpu.make_async_remote_copy(
            src_ref=src.at[other],
            dst_ref=dst.at[me],
            send_sem=send.at[0],
            recv_sem=recv.at[me],
            device_id=(g, other),
            device_id_type=MESH,
        )

    def arrived(src, dst, send, recv, t):
        other = lax.rem(me + t, n)
        pltpu.make_async_remote_copy(
            src_ref=src.at[0],
            dst_ref=dst.at[other],
            send_sem=send.at[0],
            recv_sem=recv.at[other],
            device_id=(g, other),
            device_id_type=MESH,
        ).wait_recv()

    def d_start(t, carry):
        exchange(dsend, dgot, d_send, d_recv, t).start()
        return carry

    def d_wait(t, carry):
        arrived(dsend, dgot, d_send, d_recv, t)
        return carry

    def p_start(t, carry):
        exchange(pbuf, pgot, p_send, p_recv, t).start()
        return carry

    def p_wait(t, carry):
        arrived(pbuf, pgot, p_send, p_recv, t)
        return carry

    lax.fori_loop(1, n, d_start, 0)

    @pl.when(me == n - 1)
    def _():
        cot_right[...] = jnp.zeros_like(cot_right)

    @pl.when(me < n - 1)
    def _():
        cot_copy.wait_recv()

    token = lax.broadcasted_iota(jnp.int32, (BLK, 1), 0)
    column = lax.broadcasted_iota(jnp.int32, (BLK, up.shape[0]), 1)
    jobmask = []
    live = []
    for b in range(2):
        p = plan[2 * me + b]
        jobs = job[2 * me + b]
        live.append(token < length[2 * me + b])
        own = live[b] & (p == me)
        right = live[b] & (p == me + 1)
        zero = jnp.zeros((BLK, cot.shape[1]), F32)
        block = jnp.where(
            own,
            cot[...].astype(F32),
            jnp.where(right, cot_right[...].astype(F32), zero),
        ).astype(BF16)
        dy[pl.ds(b * BLK, BLK), :] = block
        jobmask.append((column // ADAPTER_RANK == jobs).astype(F32))
        hidden[pl.ds(b * BLK, BLK), :] = (
            ADAPTER_SCALE * dot(block, up[...], 1, 1) * jobmask[b]
        ).astype(BF16)

    line = lax.broadcasted_iota(jnp.int32, (rank2, up.shape[0]), 0)
    where_col = lax.broadcasted_iota(jnp.int32, (rank2, up.shape[0]), 1)
    line_job = jnp.where(line < ADAPTER_RANK, job[2 * me], job[2 * me + 1])
    pick = (where_col == line_job * ADAPTER_RANK + line % ADAPTER_RANK).astype(F32).astype(BF16)
    same_slot = (
        lax.broadcasted_iota(jnp.int32, (rank2, tokens), 0) // ADAPTER_RANK
        == lax.broadcasted_iota(jnp.int32, (rank2, tokens), 1) // BLK
    )
    hidden_rows = jnp.where(same_slot, dot(pick, hidden[...], 1, 1), 0.0).astype(BF16)
    local[1].wait()

    def p_part(s, carry):
        pbuf[s] = dot(hidden_rows, acts[:, cols(s)], 1, 0).astype(BF16)
        return carry

    lax.fori_loop(0, n, p_part, 0)

    pgot[me] = pbuf[me]

    def z_part(d):
        for up_way in (True, False):

            @pl.when(z >= d if up_way else z + d < nz)
            def _():
                s = shard_id(z - d if up_way else z + d, y, c)
                for q in range(2):
                    w_wait(s, x, q)

                    @pl.when(z < nz - 1 if up_way else z > 0)
                    def _():
                        w_copy(
                            s,
                            x,
                            q,
                            wz_send.at[(0 if up_way else 2 * nz) + 2 * d + q],
                            to_up if up_way else to_dn,
                        ).start()

                    w_copy(s, x, q, w_send.at[0], to_x).start()
                    w_copy(s, x, q, w_send.at[1], to_y).start()
                    w_copy(s, x, q, w_send.at[2], to_s).start()

    def xy_part(d):
        for up_way in (True, False):

            @pl.when(z >= d if up_way else z + d < nz)
            def _():
                z_ = z - d if up_way else z + d
                a = shard_id(z_, y, c)
                b = shard_id(z_, 1 - y, c)
                for q in range(2):
                    w_wait(a, 1 - x, q)
                    if q == 0:
                        w_copy(a, 1 - x, q, w_send.at[1], to_y).start()
                    w_copy(a, 1 - x, q, w_send.at[2], to_s).start()
                    w_wait(b, x, q)
                    if q == 1:
                        w_copy(b, x, q, w_send.at[0], to_x).start()
                    w_copy(b, x, q, w_send.at[2], to_s).start()
                for q in range(2):
                    w_wait(b, 1 - x, q)
                    w_copy(b, 1 - x, q, w_send.at[2], to_s).start()

    acc[...] = jnp.zeros_like(acc)

    def compute(s):
        a = acts[:, cols(s)]
        w = wbuf[cols(s), :]
        acc[...] += dot(a, w, 1, 0)
        gbuf[:, cols(s)] = (dot(dy[...], w, 1, 1) + dot(hidden_rows, dgot[s], 0, 0)).astype(BF16)

    def slab(d, ways):
        def one(i, carry):
            down_way, j = i // 4, i % 4
            z_ = jnp.where(down_way == 1, z + d, z - d)
            y_ = lax.rem(y + j, 2)
            c_ = lax.rem(c + j // 2, 2)

            @pl.when((z_ >= 0) & (z_ < nz))
            def _():
                s = shard_id(z_, y_, c_)

                @pl.when(c_ != c)
                def _():
                    for h in range(2):
                        for q in range(2):
                            w_wait(s, h, q)

                compute(s)

            return carry

        lax.fori_loop(0, 4 * ways, one, 0)

    first = shard_id(z, 1 - y, c)
    for q in range(2):
        w_wait(first, x, q)
        w_copy(first, x, q, w_send.at[0], to_x).start()
        w_copy(first, x, q, w_send.at[2], to_s).start()

    if nz > 1:
        z_part(1)
    for q in range(2):
        w_wait(first, 1 - x, q)
        w_copy(first, 1 - x, q, w_send.at[2], to_s).start()

    lax.fori_loop(1, n, d_wait, 0)

    def low_part(s, total):
        return total + dot(dgot[s], acts[:, cols(s)], 1, 1)

    low = lax.fori_loop(0, n, low_part, jnp.zeros((rank2, tokens), F32))
    low_rows = jnp.where(same_slot, low, 0.0).astype(BF16)
    up_part = (ADAPTER_SCALE * dot(low_rows, dy[...], 1, 0)).astype(BF16)
    width = up_part.shape[1] // REDUCERS
    every = n // REDUCERS
    for k in range(REDUCERS):
        ubuf[k] = up_part[:, k * width : (k + 1) * width]
    for k in range(REDUCERS):

        @pl.when(me == k * every)
        def _():
            ugot[me] = ubuf[k]

        @pl.when(me != k * every)
        def _():
            pltpu.make_async_remote_copy(
                src_ref=ubuf.at[k],
                dst_ref=ugot.at[me],
                send_sem=u_send.at[k],
                recv_sem=u_recv.at[me],
                device_id=(g, k * every),
                device_id_type=MESH,
            ).start()

    slab(0, 1)

    def t_copy(k, other):
        return pltpu.make_async_remote_copy(
            src_ref=utotal.at[k],
            dst_ref=utotal.at[k],
            send_sem=t_send.at[0],
            recv_sem=t_recv.at[k],
            device_id=(g, other),
            device_id_type=MESH,
        )

    def reduce_up():
        def u_wait(t, carry):
            other = lax.rem(me + t, n)
            pltpu.make_async_remote_copy(
                src_ref=ubuf.at[0],
                dst_ref=ugot.at[other],
                send_sem=u_send.at[0],
                recv_sem=u_recv.at[other],
                device_id=(g, other),
                device_id_type=MESH,
            ).wait_recv()
            return carry

        lax.fori_loop(1, n, u_wait, 0)
        k = me // every
        utotal[k] = dot(hot, ugot[...].reshape(n * rank2, width), 1, 0).astype(BF16)

        def t_start(t, carry):
            t_copy(k, lax.rem(me + t, n)).start()
            return carry

        lax.fori_loop(1, n, t_start, 0)

    def step(d, carry):
        @pl.when(d + 1 < nz)
        def _():
            z_part(d + 1)

        @pl.when(d == nz - 2)
        def _():
            lax.fori_loop(1, n, p_start, 0)

        xy_part(d)

        @pl.when((d == nz - 1) & (me % every == 0))
        def _():
            reduce_up()

        slab(d, 2)
        return carry

    lax.fori_loop(1, nz, step, 0)


    up_rows = dot(pick, up[...], 1, 0).astype(BF16)
    whole = acc[...] + ADAPTER_SCALE * dot(low_rows, up_rows, 0, 0)
    keep = jnp.zeros((BLK, up.shape[1]), F32)
    give = keep
    for b in range(2):
        p = plan[2 * me + b]
        block = whole[b * BLK : (b + 1) * BLK]
        keep = jnp.where(live[b] & (p == me), block, keep)
        give = jnp.where(live[b] & (p == me + 1), block, give)
    vsend[...] = give.astype(BF16)
    val_copy = pltpu.make_async_remote_copy(
        src_ref=vsend,
        dst_ref=vgot,
        send_sem=val_sem.at[0],
        recv_sem=val_sem.at[1],
        device_id=(g, jnp.minimum(me + 1, n - 1)),
        device_id_type=MESH,
    )

    @pl.when(me < n - 1)
    def _():
        val_copy.start()

    lax.fori_loop(1, n, p_wait, 0)
    down_out[...] = dot(pgot[...].reshape(n * rank2, rows), hot, 0, 1)

    for k in range(REDUCERS):

        @pl.when(me != k * every)
        def _():
            t_copy(k, k * every).wait_recv()

        up_out[:, k * width : (k + 1) * width] = utotal[k].astype(F32)

    def drain(ref, sem):
        pltpu.make_async_copy(ref, ref, sem).wait()

    drain(wbuf.at[pl.ds(0, (3 * nz - 1) * piece)], w_send.at[0])
    drain(wbuf.at[pl.ds(0, (3 * nz - 1) * piece)], w_send.at[1])
    drain(wbuf.at[pl.ds(0, n // 2 * rows)], w_send.at[2])
    drain(dsend.at[pl.ds(0, n - 1)], d_send.at[0])
    drain(pbuf.at[pl.ds(0, n - 1)], p_send.at[0])

    for d in range(nz):
        for up_way in (True, False):

            @pl.when((z >= d) & (z < nz - 1) if up_way else (z + d < nz) & (z > 0))
            def _():
                s = shard_id(z - d if up_way else z + d, y, c)
                base = 0 if up_way else nz
                for q in range(2):
                    w_copy(s, x, q, wz_send.at[2 * base + 2 * d + q], to_y).wait_send()

    for k in range(REDUCERS):

        @pl.when(me != k * every)
        def _():
            drain(ubuf.at[k], u_send.at[k])

    @pl.when(me % every == 0)
    def _():
        drain(wbuf.at[pl.ds(0, (n - 1) * up.shape[0] // REDUCERS)], t_send.at[0])

    @pl.when(me > 0)
    def _():
        cot_copy.wait_send()


    @pl.when(me < n - 1)
    def _():
        val_copy.wait_send()

    @pl.when(me == 0)
    def _():
        values_out[...] = keep.astype(BF16)

    @pl.when(me > 0)
    def _():
        val_copy.wait_recv()
        values_out[...] = (keep + vgot[...].astype(F32)).astype(BF16)


def body(
    n,
    acts,
    cotangent,
    plan,
    source_block_length,
    source_block_job,
    frozen_value_weight,
    adapter_down_weight,
    adapter_up_weight,
):
    tokens, features = acts.shape
    rows, out_width = frozen_value_weight.shape
    job_columns = adapter_down_weight.shape[1]
    rank2 = 2 * ADAPTER_RANK
    width = out_width // REDUCERS
    codes = (
        source_block_job[:, None] * ADAPTER_RANK + jnp.arange(ADAPTER_RANK, dtype=jnp.int32)[None]
    ).reshape(1, -1)
    smem = pl.BlockSpec(memory_space=pltpu.SMEM)
    vmem = pl.BlockSpec(memory_space=pltpu.VMEM)
    anywhere = pl.BlockSpec(memory_space=pl.ANY)
    dma = pltpu.SemaphoreType.DMA
    nz = n // 4
    return pl.pallas_call(
        functools.partial(kernel, n),
        out_shape=(
            jax.ShapeDtypeStruct((BLK, out_width), BF16),
            pltpu.VMEM((tokens, features), BF16),
            jax.ShapeDtypeStruct((rows, job_columns), F32),
            jax.ShapeDtypeStruct((job_columns, out_width), F32),
        ),
        in_specs=[smem, smem, smem, vmem, anywhere, vmem, anywhere, vmem, vmem],
        out_specs=(vmem, vmem, vmem, vmem),
        scratch_shapes=[
            pltpu.VMEM((tokens, features), BF16),
            pltpu.VMEM((n * rows, out_width), BF16),
            pltpu.VMEM((n, rank2, rows), BF16),
            pltpu.VMEM((n, rank2, rows), BF16),
            pltpu.VMEM((BLK, out_width), BF16),
            pltpu.VMEM((tokens, out_width), BF16),
            pltpu.VMEM((tokens, job_columns), BF16),
            pltpu.VMEM((tokens, out_width), F32),
            pltpu.VMEM((n, rank2, rows), BF16),
            pltpu.VMEM((n, rank2, rows), BF16),
            pltpu.VMEM((REDUCERS, rank2, width), BF16),
            pltpu.VMEM((n, rank2, width), BF16),
            pltpu.VMEM((REDUCERS, job_columns, width), BF16),
            pltpu.VMEM((BLK, out_width), BF16),
            pltpu.VMEM((BLK, out_width), BF16),
            dma((2,)),
            dma((2,)),
            dma((2,)),
            dma((n * 4,)),
            dma((3,)),
            dma((4 * nz,)),
            dma((n,)),
            dma((1,)),
            dma((1,)),
            dma((n,)),
            dma((REDUCERS,)),
            dma((n,)),
            dma((1,)),
            dma((REDUCERS,)),
        ],
        compiler_params=pltpu.CompilerParams(
            collective_id=0, has_side_effects=True, vmem_limit_bytes=57 * 1024 * 1024
        ),
        cost_estimate=pl.CostEstimate(
            flops=4 * tokens * features * out_width,
            bytes_accessed=4 * tokens * features,
            transcendentals=0,
        ),
    )(
        plan,
        source_block_length,
        source_block_job,
        codes,
        acts,
        cotangent,
        frozen_value_weight,
        adapter_down_weight,
        adapter_up_weight,
    )


def solution(mesh):
    placed = (
        P(("groups", "fsdp"), None),
        P(("groups", "fsdp"), None),
        P("groups"),
        P("groups"),
        P("groups"),
        P("fsdp", None),
        P(("groups", "fsdp"), None),
        P("groups", None),
    )
    return jax.shard_map(
        functools.partial(body, mesh.shape["fsdp"]),
        mesh=mesh,
        in_specs=placed,
        out_specs=(
            P(("groups", "fsdp"), None),
            P(("groups", "fsdp"), None),
            P(("groups", "fsdp"), None),
            P("groups", None),
        ),
        check_vma=False,
    )
```
